256 devices in a mesh: dp: 8 (over z), eslice: 32 (over x, y, core).
Axes of the slice: x: 4, y: 4, z: 8, core: 2. Of those that a mesh axis runs over, the one named last changes fastest.
Arguments:
- inputs: bfloat16 [32768, 2048], P(('dp', 'eslice')), may hold values from -6 to 6
- cotangent: bfloat16 [32768, 2048], P(('dp', 'eslice')), may hold values from -6 to 6
- routes: int32 [32768, 2], P(('dp', 'eslice')), may hold values from 0 to 15, all different within a row; in each aligned block of 128 rows (0 to 127, 128 to 255, ...) at most 20 rows name the same one
- gate_weights: bfloat16 [32768, 2], P(('dp', 'eslice')), may hold values from 0.049804688 to 1
- gate_weight: bfloat16 [64, 2048, 256], P('eslice', 'dp'), may hold values from -0.125 to 0.125
- up_weight: bfloat16 [64, 2048, 256], P('eslice', 'dp'), may hold values from -0.125 to 0.125
- down_weight: bfloat16 [64, 2048, 256], P('eslice', 'dp'), may hold values from -0.09375 to 0.09375
Outputs:
- input_grad: bfloat16 [32768, 2048], P(('dp', 'eslice'))
- gate_grad: float32 [32768, 2], P(('dp', 'eslice'))
- gate_weight_grad: bfloat16 [64, 2048, 256], P('eslice', 'dp')
- up_weight_grad: bfloat16 [64, 2048, 256], P('eslice', 'dp')
- down_weight_grad: bfloat16 [64, 2048, 256], P('eslice', 'dp')
The draws below stay inside these ranges and needn't reach their ends.
Inputs may be any that keep to these rules, and one draw needn't show every extreme that they name: In the 256 routes of one device's tokens no expert is named more than 20 times, a bound that some block reaches; a token's 2 experts differ; every expert is named somewhere.
All inputs are finite; a program needn't handle non-finite values.
Results may differ from the reference program's by a relative error of at most 0.017.
Values may be sent and summed in bfloat16 or wider, within the bound.
No kernel may reach another device: no remote copies, remote signals or barrier semaphores. Data moves between devices by JAX's collectives and lax.ppermute only.
A program may use at most 128 MiB of HBM per device.

```python
import math
import jax
import jax.numpy as jnp
import numpy as np
from jax import lax

D = 2048
FF = 1024
SLICES = 4
EXP_LOCAL = 2
TOPK = 2
TOK_DEV = 128
GROUPS = 8
EXPERTS = 16
CAP = 20
TOKENS = 32768
N_DP = 8


def levels(rng, extent, split, low, high):
    factor_of, own = 1.0, jax.random.fold_in(rng, 6)
    for axis_at, parts in split:
        steps = jnp.exp(jax.random.uniform(jax.random.fold_in(own, axis_at), (parts,), jnp.float32, low / len(split), high / len(split)))
        factor_of = factor_of * jnp.repeat(steps, extent[axis_at] // parts).reshape([-1 if axis == axis_at else 1 for axis in range(len(extent))])
    return factor_of


def routed_block(own_key, own, number, rows, amount, top, reach, slope):
    ranking = jax.random.permutation(own_key, amount)
    crowded, ordinary = portions_of(amount, rows * top, reach, slope, True), portions_of(amount, rows * top, reach, slope, False)
    places = jnp.arange(amount)

    def named(tallies, offset_by):
        used = int((tallies > 0).sum())
        fixed = max(1, used // 4)
        shifted = fixed + (places - fixed + offset_by * (used - fixed)) % max(1, amount - fixed)
        return jnp.zeros((amount,), jnp.int32).at[ranking[jnp.where(places < fixed, places, shifted)]].set(jnp.asarray(tallies, jnp.int32))

    tallies = jnp.where(number % 4 == 0, named(crowded, number // 4), named(ordinary, number - number // 4 - 1))
    mixed = jax.random.permutation(jax.random.fold_in(own, 3), amount)
    giver, sink = mixed[0:amount // 2 * 2:2], mixed[1:amount // 2 * 2:2]
    room = jnp.minimum(tallies[giver] - 1, reach - tallies[sink]) // 2
    room = jnp.where((giver == ranking[0]) | (sink == ranking[0]) | (tallies[sink] == 0), 0, jnp.maximum(room, 0))
    shifted = jax.random.randint(jax.random.fold_in(own, 4), (amount // 2,), 0, 1 << 20) % (room + 1)
    tallies = tallies.at[giver].add(-shifted).at[sink].add(shifted)
    members = jnp.searchsorted(jnp.cumsum(tallies), jnp.arange(rows * top), side="right").astype(jnp.int32)
    table = members.reshape(top, rows).T
    table = table[jax.random.permutation(jax.random.fold_in(own, 1), rows)]
    offset_by = jax.random.randint(jax.random.fold_in(own, 2), (rows, 1), 0, top)
    return jnp.take_along_axis(table, (jnp.arange(top)[None, :] + offset_by) % top, axis=1)


def portions_of(count, total, most, skew, full):
    loads = [(1 << 20) // math.isqrt(grade ** skew) + 1 for grade in range(1, count + 1)]
    largest = most if full else min(most, max(-(-total // count), total * loads[0] // sum(loads)))
    least = 1 if total - largest >= count - 1 else 0
    given, rest = [largest] + [least] * (count - 1), total - largest - least * (count - 1)
    while rest > 0:
        free = [i for i in range(1, count) if given[i] < largest] or [i for i in range(1, count) if given[i] < most]
        pool, left = sum([loads[i] for i in free]), rest
        for i in free:
            more = min(most - given[i], max(1, left * loads[i] // pool), rest)
            given[i] = given[i] + more
            rest = rest - more
    return np.array(given)


def bell_draw(rng, extent, width, bound, split=(), kind=jnp.bfloat16):
    gain = levels(rng, extent, split, -0.22, 0.18) if split else 1.0
    entries = jax.random.normal(rng, extent, jnp.float32) * width * gain
    return jnp.minimum(jnp.maximum(entries, -bound), bound).astype(kind)


def setup_inputs(seed: int = 0) -> dict:
    arg_keys = jax.random.split(jax.random.key(seed), 8)
    inputs = bell_draw(arg_keys[0], (TOKENS, D), 1.0, 6.0, ((0, 256),))
    cotangent = bell_draw(arg_keys[1], (TOKENS, D), 1.0, 6.0, ((0, 256),))
    routes_keys = jax.random.split(jax.random.fold_in(arg_keys[2], 1), TOKENS // TOK_DEV)
    routes_turns = jax.random.permutation(jax.random.fold_in(arg_keys[2], 3), TOKENS // TOK_DEV)
    routes = jax.vmap(lambda own, number: routed_block(jax.random.fold_in(arg_keys[2], 2), own, number, TOK_DEV, EXPERTS, TOPK, CAP, 2))(routes_keys, routes_turns).reshape((TOKENS, TOPK))
    gate_weights = jnp.clip(0.049804688 + 0.9501953 * jax.random.uniform(arg_keys[3], (TOKENS, TOPK), jnp.float32) ** levels(arg_keys[3], (TOKENS, TOPK), ((0, 256),), -0.2, 0.2), 0.049804688, 1.0).astype(jnp.bfloat16)
    gate_weight = bell_draw(arg_keys[4], (EXPERTS * SLICES, D, FF // SLICES), D ** -0.5, 0.125, ((0, 32), (1, 8)))
    up_weight = bell_draw(arg_keys[5], (EXPERTS * SLICES, D, FF // SLICES), D ** -0.5, 0.125, ((0, 32), (1, 8)))
    down_weight = bell_draw(arg_keys[6], (EXPERTS * SLICES, D, FF // SLICES), (4 * FF) ** -0.5, 0.09375, ((0, 32), (1, 8)))
    return {"inputs": inputs, "cotangent": cotangent, "routes": routes, "gate_weights": gate_weights, "gate_weight": gate_weight, "up_weight": up_weight, "down_weight": down_weight}


def slot_owner(block_routes):
    flat = block_routes.reshape(-1)
    count = flat.shape[0]
    onehot = (flat[:, None] == jnp.arange(EXPERTS, dtype=jnp.int32)[None, :]).astype(jnp.int32)
    position = jnp.sum(jnp.cumsum(onehot, axis=0) * onehot, axis=1) - 1
    target = flat * CAP + position
    owner = jnp.full((EXPERTS * CAP,), -1, jnp.int32)
    return owner.at[target].set(jnp.arange(count, dtype=jnp.int32))


def assemble(stored):
    shaped = stored.reshape(GROUPS, SLICES, EXP_LOCAL, D, FF // SLICES)
    return shaped.transpose(0, 2, 3, 1, 4).reshape(EXPERTS, D, FF)


def disassemble(whole):
    shaped = whole.reshape(GROUPS, EXP_LOCAL, D, SLICES, FF // SLICES)
    return shaped.transpose(0, 3, 1, 2, 4).reshape(EXPERTS * SLICES, D, FF // SLICES)


def rounded_sum(values, axis):
    narrow = lax.optimization_barrier(values.astype(jnp.bfloat16))
    return jnp.sum(narrow.astype(jnp.float32), axis=axis)


def reference(inputs, cotangent, routes, gate_weights, gate_weight, up_weight, down_weight):
    blocks = TOKENS // TOK_DEV
    pairs = TOK_DEV * TOPK
    quarter_width = FF // SLICES
    owners = jax.vmap(slot_owner)(routes.reshape(blocks, TOK_DEV, TOPK))
    owners = owners.reshape(blocks, EXPERTS, CAP).transpose(1, 0, 2)
    offsets = (jnp.arange(blocks, dtype=jnp.int32) * pairs)[:, None]
    flat_gates = gate_weights.reshape(-1)
    row_count = blocks * CAP

    def weight_part(left, right):
        left_wide = left.astype(jnp.float32).reshape(N_DP, row_count // N_DP, D)
        right_wide = right.astype(jnp.float32).reshape(N_DP, row_count // N_DP, FF)
        return rounded_sum(jnp.einsum("ird,irf->idf", left_wide, right_wide), 0).astype(jnp.bfloat16)

    def per_expert(carry, items):
        grad_acc, gate_acc = carry
        owner, gate_slab, up_slab, down_slab = items
        valid = (owner >= 0).reshape(-1)
        pair_index = jnp.where(owner >= 0, offsets + owner, 0).reshape(-1).astype(jnp.int32)
        token_index = pair_index // TOPK
        rows_in = jnp.where(valid[:, None], inputs[token_index], 0)
        rows_dy = jnp.where(valid[:, None], cotangent[token_index], 0)
        gate_scale = jnp.where(valid, flat_gates[pair_index].astype(jnp.float32), 0.0)
        gate_pre = jnp.dot(rows_in, gate_slab, preferred_element_type=jnp.float32)
        up_pre = jnp.dot(rows_in, up_slab, preferred_element_type=jnp.float32)
        projected = jnp.dot(rows_dy, down_slab, preferred_element_type=jnp.float32)
        sigmoid_gate = jax.nn.sigmoid(gate_pre)
        hidden = (gate_pre * sigmoid_gate * up_pre).astype(jnp.bfloat16)
        hidden_wide = hidden.astype(jnp.float32)
        quarter = jnp.sum((hidden_wide * projected).reshape(row_count, SLICES, quarter_width), axis=2)
        gate_part = rounded_sum(quarter, 1)
        hidden_grad = gate_scale[:, None] * projected
        dgate_pre = (hidden_grad * up_pre * sigmoid_gate * (1.0 + gate_pre * (1.0 - sigmoid_gate))).astype(jnp.bfloat16)
        dup_pre = (hidden_grad * gate_pre * sigmoid_gate).astype(jnp.bfloat16)
        scaled_hidden = (gate_scale[:, None] * hidden_wide).astype(jnp.bfloat16)
        split_gate = dgate_pre.astype(jnp.float32).reshape(row_count, SLICES, quarter_width)
        split_up = dup_pre.astype(jnp.float32).reshape(row_count, SLICES, quarter_width)
        gate_wide = gate_slab.astype(jnp.float32).reshape(D, SLICES, quarter_width)
        up_wide = up_slab.astype(jnp.float32).reshape(D, SLICES, quarter_width)
        partial_value = jnp.einsum("rsf,dsf->rsd", split_gate, gate_wide) + jnp.einsum("rsf,dsf->rsd", split_up, up_wide)
        grad_rows = rounded_sum(partial_value, 1)
        grad_acc = grad_acc.at[token_index].add(grad_rows)
        gate_acc = gate_acc.at[pair_index].add(gate_part)
        grads = (weight_part(rows_in, dgate_pre), weight_part(rows_in, dup_pre), weight_part(rows_dy, scaled_hidden))
        return (grad_acc, gate_acc), grads

    start_state = (jnp.zeros((TOKENS, D), jnp.float32), jnp.zeros((TOKENS * TOPK,), jnp.float32))
    slabs = (owners, assemble(gate_weight), assemble(up_weight), assemble(down_weight))
    (grad_acc, gate_acc), (gate_grads, up_grads, down_grads) = lax.scan(per_expert, start_state, slabs)
    return (grad_acc.astype(jnp.bfloat16), gate_acc.reshape(TOKENS, TOPK),
            disassemble(gate_grads), disassemble(up_grads), disassemble(down_grads))
```

```python
import functools

import jax
import jax.numpy as jnp
from jax import lax
from jax.experimental import pallas as pl
from jax.experimental.pallas import tpu as pltpu
from jax.sharding import PartitionSpec as P

BF = jnp.bfloat16
F32 = jnp.float32
T = 128
D = 2048
E = 16
SRC = 32
MAIN = 16
REST = 4
ROWS = SRC * (MAIN + REST)
FULL = SRC * MAIN
CB = 256
MB = 1 << 20


def iota(shape, dim):
    return lax.broadcasted_iota(jnp.int32, shape, dim)


def dot(a, b, ca=1, cb=0):
    return lax.dot_general(a, b, (((ca,), (cb,)), ((), ())), preferred_element_type=F32)


def slots(routes):
    lane = iota((T, 128), 1)
    first = routes[:, 0:1] == lane
    second = routes[:, 1:2] == lane
    member = jnp.logical_or(first, second)
    before = (iota((T, T), 1) < iota((T, T), 0)).astype(BF)
    position = dot(before, member.astype(F32).astype(BF))
    return first, second, jnp.where(member, position, -1.0)


def send_kernel(routes_ref, gates_ref, x_ref, dy_ref, sx_ref, sdy_ref):
    first, second, slot = slots(routes_ref[...])
    gates = gates_ref[...].astype(F32)
    gate = jnp.where(first, gates[:, 0:1], 0.0) + jnp.where(second, gates[:, 1:2], 0.0)
    count = E * MAIN
    expand = (iota((count, 128), 0) // MAIN == iota((count, 128), 1)).astype(F32).astype(BF)
    slot_row = dot(expand, slot.T.astype(BF))
    gate_row = dot(expand, gate.T.astype(BF))
    row = iota((count, T), 0)
    main = slot_row == (row % MAIN).astype(F32)
    rest = slot_row == (row % REST + MAIN).astype(F32)
    block = row // REST % 4

    def emit(values, src_ref, out_ref):
        pick = jnp.where(main, values, 0.0).astype(BF)
        picks = [jnp.where(jnp.logical_and(rest, block == k), values, 0.0).astype(BF) for k in range(4)]
        for half in range(2):
            left = None
            for k in range(4):
                cols = src_ref[:, half * 1024 + k * CB:half * 1024 + (k + 1) * CB]
                got = dot(pick, cols).astype(BF)
                out_ref[:, half, k * MAIN:(k + 1) * MAIN, :] = got.reshape(E, MAIN, CB)
                more = dot(picks[k], cols)
                left = more if left is None else left + more
            out_ref[:, half, 4 * MAIN:5 * MAIN, :] = left.astype(BF).reshape(E, MAIN, CB)

    emit(jnp.ones((count, T), F32), x_ref, sx_ref)
    emit(gate_row, dy_ref, sdy_ref)


def rest_pick(k):
    shape = (SRC * REST, FULL)
    r, c = iota(shape, 0), iota(shape, 1)
    hit = jnp.logical_and(r // REST == c // MAIN, r % REST == c % REST)
    return jnp.logical_and(hit, c // REST % 4 == k).astype(F32).astype(BF)


def assemble_kernel(core_ref, mine_ref, other_ref, out_ref):
    core = core_ref[0]
    for ref, half in ((mine_ref, core), (other_ref, 1 - core)):
        left = ref[:, 4 * MAIN:5 * MAIN, :].reshape(FULL, CB)
        for k in range(4):
            cols = pl.ds(pl.multiple_of(half * 1024 + k * CB, CB), CB)
            out_ref[0:FULL, cols] = ref[:, k * MAIN:(k + 1) * MAIN, :].reshape(FULL, CB)
            out_ref[FULL:ROWS, cols] = dot(rest_pick(k), left).astype(BF)


def main_kernel(x_ref, dy_ref, w_ref, dgate_ref, dup_ref, gate_ref, grad_ref, hid_ref):
    q = pl.program_id(0)
    step = 128
    wg = w_ref[:, 0, 0].reshape(D, CB)
    wu = w_ref[:, 0, 1].reshape(D, CB)
    wd = w_ref[:, 0, 2].reshape(D, CB)
    for at in range(0, ROWS, step):
        rows = slice(at, at + step)
        gpre = dot(x_ref[rows, :], wg)
        upre = dot(x_ref[rows, :], wu)
        zeta = dot(dy_ref[rows, :], wd)
        sig = jax.nn.sigmoid(gpre)
        act = gpre * sig
        hidden = (act * upre).astype(BF)
        hid_ref[rows, :] = hidden
        part = jnp.sum(hidden.astype(F32) * zeta, axis=1, keepdims=True)
        part = jnp.broadcast_to(part, (step, 128))

        @pl.when(q == 0)
        def _():
            gate_ref[rows, :] = part

        @pl.when(q != 0)
        def _():
            gate_ref[rows, :] += part

        dgate_ref[0, rows, :] = (zeta * upre * sig * (1.0 + gpre * (1.0 - sig))).astype(BF)
        dup_ref[0, rows, :] = (zeta * act).astype(BF)
    for m, (left, right) in enumerate(
        ((dgate_ref[0], x_ref), (dup_ref[0], x_ref), (hid_ref[...], dy_ref))
    ):
        for d in range(8):
            grad_ref[d, 0, m] = dot(left, right[:, d * CB:(d + 1) * CB], 0, 0).astype(BF)


def back_kernel(dgate_ref, dup_ref, gate_ref, w_ref, out_ref):
    picks = [rest_pick(k) for k in range(4)]
    for group in range(2):
        left = None
        for k in range(4):
            d = group * 4 + k
            total = None
            for q in range(2):
                a = dot(dgate_ref[q], w_ref[d, q, 0], 1, 1)
                b = dot(dup_ref[q], w_ref[d, q, 1], 1, 1)
                total = a + b if total is None else total + a + b
            rows = total.astype(BF)
            out_ref[:, d * MAIN:(d + 1) * MAIN, :] = rows[0:FULL].reshape(SRC, MAIN, CB)
            more = dot(picks[k], rows[FULL:ROWS], 0, 0)
            left = more if left is None else left + more
        at = (8 + group) * MAIN
        out_ref[:, at:at + MAIN, :] = left.astype(BF).reshape(SRC, MAIN, CB)
    gates = gate_ref[...].astype(BF)
    out_ref[:, 10 * MAIN:11 * MAIN, 0:128] = gates[0:FULL].reshape(SRC, MAIN, 128)
    spread = dot(picks[0], gates[FULL:ROWS], 0, 0).astype(BF)
    out_ref[:, 10 * MAIN:11 * MAIN, 128:256] = spread.reshape(SRC, MAIN, 128)


def combine_kernel(routes_ref, gates_ref, back_ref, grad_ref, gate_ref):
    first, second, slot = slots(routes_ref[...])
    gates = gates_ref[...].astype(F32)
    count = 2 * E * MAIN
    expand = (iota((128, count), 1) // (2 * MAIN) == iota((128, count), 0)).astype(F32).astype(BF)
    col = iota((T, count), 1)
    main_at = (col % MAIN).astype(F32)
    rest_at = (col % REST + MAIN).astype(F32)
    block = col // REST % 4
    slot_col = dot(slot.astype(BF), expand)
    main = (slot_col == main_at).astype(F32).astype(BF)
    rest = slot_col == rest_at
    rests = [jnp.logical_and(rest, block == k).astype(F32).astype(BF) for k in range(4)]
    for d in range(8):
        got = back_ref[:, d * MAIN:(d + 1) * MAIN, :].reshape(count, CB)
        at = (8 + d // 4) * MAIN
        more = back_ref[:, at:at + MAIN, :].reshape(count, CB)
        grad_ref[:, d * CB:(d + 1) * CB] = (dot(main, got) + dot(rests[d % 4], more)).astype(BF)
    parts = back_ref[:, 10 * MAIN:11 * MAIN, :].reshape(count, CB)
    columns = []
    for k, chosen in enumerate((first, second)):
        own = dot(jnp.where(chosen, slot, -1.0).astype(BF), expand)
        own = jnp.where(dot(chosen.astype(F32).astype(BF), expand) > 0.5, own, -1.0)
        a = (own == main_at).astype(F32).astype(BF)
        b = jnp.logical_and(own == rest_at, block == 0).astype(F32).astype(BF)
        value = dot(a, parts[:, 0:128]) + dot(b, parts[:, 128:256])
        columns.append(value[:, 0:1] / gates[:, k:k + 1])
    gate_ref[...] = jnp.concatenate(columns, axis=1)


def vmem(count):
    return [pl.BlockSpec(memory_space=pltpu.VMEM)] * count


def params():
    return pltpu.CompilerParams(vmem_limit_bytes=48 * MB)


def cost(flops, moved):
    return pl.CostEstimate(flops=flops, bytes_accessed=moved, transcendentals=0)


def shape(*sizes, dtype=BF):
    return jax.ShapeDtypeStruct(sizes, dtype)


def per_device(inputs, cotangent, routes, gate_weights, gate_weight, up_weight, down_weight):
    here = lax.axis_index("eslice")
    core = here % 2
    side = here // 2 % 2

    stacked = jnp.stack((gate_weight, up_weight, down_weight), axis=1)
    own = lax.dynamic_index_in_dim(stacked, side, 0, keepdims=False)
    away = lax.dynamic_index_in_dim(stacked, 1 - side, 0, keepdims=False)
    swap = [(i, i ^ 2) for i in range(SRC)]
    partner = [(i, i ^ 1) for i in range(SRC)]
    came = lax.ppermute(away, "eslice", swap)
    weights = lax.all_gather(jnp.stack((own, came)), "dp", axis=0, tiled=False)

    send_x, send_dy = pl.pallas_call(
        send_kernel,
        out_shape=(shape(E, 2, 5 * MAIN, CB), shape(E, 2, 5 * MAIN, CB)),
        in_specs=vmem(4),
        out_specs=tuple(vmem(2)),
        compiler_params=params(),
        cost_estimate=cost(10**9, 4 * MB),
        name="send",
    )(routes, gate_weights, inputs, cotangent)

    def dispatch(values):
        mine = lax.all_to_all(values.reshape(SRC, 5 * MAIN, CB), "eslice", 0, 0, tiled=True)
        other = lax.ppermute(mine, "eslice", partner)
        return pl.pallas_call(
            assemble_kernel,
            out_shape=shape(ROWS, D),
            in_specs=[pl.BlockSpec(memory_space=pltpu.SMEM)] + vmem(2),
            out_specs=pl.BlockSpec(memory_space=pltpu.VMEM),
            compiler_params=params(),
            cost_estimate=cost(10**9, 5 * MB),
            name="assemble",
        )(core.reshape(1), mine, other)

    rows_x = dispatch(send_x)
    rows_dy = dispatch(send_dy)

    dgate, dup, gate_part, grads = pl.pallas_call(
        main_kernel,
        grid=(2,),
        out_shape=(
            shape(2, ROWS, CB),
            shape(2, ROWS, CB),
            shape(ROWS, 128, dtype=F32),
            shape(8, 2, 3, CB, CB),
        ),
        in_specs=[
            pl.BlockSpec((ROWS, D), lambda q: (0, 0)),
            pl.BlockSpec((ROWS, D), lambda q: (0, 0)),
            pl.BlockSpec((8, 1, 3, CB, CB), lambda q: (0, q, 0, 0, 0)),
        ],
        out_specs=(
            pl.BlockSpec((1, ROWS, CB), lambda q: (q, 0, 0)),
            pl.BlockSpec((1, ROWS, CB), lambda q: (q, 0, 0)),
            pl.BlockSpec((ROWS, 128), lambda q: (0, 0)),
            pl.BlockSpec((8, 1, 3, CB, CB), lambda q: (0, q, 0, 0, 0)),
        ),
        scratch_shapes=[pltpu.VMEM((ROWS, CB), BF)],
        compiler_params=params(),
        cost_estimate=cost(8 * 10**9, 20 * MB),
        name="main",
    )(rows_x, rows_dy, weights)

    back = pl.pallas_call(
        back_kernel,
        out_shape=shape(SRC, 11 * MAIN, CB),
        in_specs=vmem(4),
        out_specs=pl.BlockSpec(memory_space=pltpu.VMEM),
        compiler_params=params(),
        cost_estimate=cost(3 * 10**9, 10 * MB),
        name="back",
    )(dgate, dup, gate_part, weights)
    returned = lax.all_to_all(back, "eslice", 0, 0, tiled=True)
    input_grad, gate_grad = pl.pallas_call(
        combine_kernel,
        out_shape=(shape(T, D), shape(T, 2, dtype=F32)),
        in_specs=vmem(3),
        out_specs=tuple(vmem(2)),
        compiler_params=params(),
        cost_estimate=cost(10**9, 4 * MB),
        name="combine",
    )(routes, gate_weights, returned)

    reduced = lax.psum_scatter(grads, "dp", scatter_dimension=0, tiled=False)
    kept = reduced[0]
    came = lax.ppermute(reduced[1], "eslice", swap)
    low = jnp.where(side == 0, kept, came)
    high = jnp.where(side == 0, came, kept)
    out = jnp.stack((low, high), axis=1).swapaxes(2, 3)
    return (input_grad, gate_grad, out[0], out[1], out[2])


def solution(mesh):
    token = P(("dp", "eslice"), None)
    weight = P("eslice", "dp", None)
    return jax.shard_map(
        per_device,
        mesh=mesh,
        in_specs=(token,) * 4 + (weight,) * 3,
        out_specs=(token,) * 2 + (weight,) * 3,
        check_vma=False,
    )
```

```python
import functools

import jax
import jax.numpy as jnp
from jax import lax
from jax.experimental import pallas as pl
from jax.experimental.pallas import tpu as pltpu
from jax.sharding import PartitionSpec as P

BF = jnp.bfloat16
F32 = jnp.float32
T = 128
D = 2048
E = 16
SRC = 32
MAIN = 16
REST = 4
ROWS = SRC * (MAIN + REST)
FULL = SRC * MAIN
CB = 256
MB = 1 << 20


def iota(shape, dim):
    return lax.broadcasted_iota(jnp.int32, shape, dim)


def dot(a, b, ca=1, cb=0):
    return lax.dot_general(a, b, (((ca,), (cb,)), ((), ())), preferred_element_type=F32)


def slots(routes):
    expert = iota((128, T), 0)
    first = routes[0:1, :] == expert
    second = routes[1:2, :] == expert
    member = jnp.logical_or(first, second)
    before = (iota((T, T), 0) < iota((T, T), 1)).astype(F32).astype(BF)
    position = dot(member.astype(F32).astype(BF), before)
    return first, second, jnp.where(member, position, -1.0)


def send_kernel(routes_ref, gates_ref, x_ref, dy_ref, out_ref):
    first, second, slot = slots(routes_ref[...])
    gates = gates_ref[...].astype(F32)
    gate = jnp.where(first, gates[0:1, :], 0.0) + jnp.where(second, gates[1:2, :], 0.0)
    count = E * MAIN
    expand = (iota((count, 128), 0) // MAIN == iota((count, 128), 1)).astype(F32).astype(BF)
    slot_row = dot(expand, slot.astype(BF))
    gate_row = dot(expand, gate.astype(BF))
    row = iota((count, T), 0)
    main = slot_row == (row % MAIN).astype(F32)
    rest = slot_row == (row % REST + MAIN).astype(F32)
    block = row // REST % 4

    def put(at, rows):
        rows = rows.astype(BF).reshape(E // 2, 2, MAIN, CB)
        for side in range(2):
            out_ref[:, side, :, at * MAIN:(at + 1) * MAIN, :] = rows

    for base, values, src_ref in ((0, 1.0, x_ref), (10, gate_row, dy_ref)):
        pick = jnp.where(main, values, 0.0).astype(BF)
        picks = [jnp.where(jnp.logical_and(rest, block == k), values, 0.0).astype(BF) for k in range(4)]
        for group in range(2):
            left = None
            for k in range(4):
                d = group * 4 + k
                cols = src_ref[:, d * CB:(d + 1) * CB]
                put(base + d, dot(pick, cols))
                more = dot(picks[k], cols)
                left = more if left is None else left + more
            put(base + 8 + group, left)


def rest_pick(k):
    shape = (SRC * REST, FULL)
    r, c = iota(shape, 0), iota(shape, 1)
    hit = jnp.logical_and(r // REST == c // MAIN, r % REST == c % REST)
    return jnp.logical_and(hit, c // REST % 4 == k).astype(F32).astype(BF)


def pack_kernel(core_ref, *refs):
    for i, ref in enumerate(refs[:6]):
        refs[6][i // 3, i % 3] = ref[core_ref[0]]


def unpack(rows_in, base, into, left_ref, sem):
    copies = []
    for d in range(8):
        copies.append(pltpu.make_async_copy(
            rows_in.at[:, pl.ds((base + d) * MAIN, MAIN)],
            into.at[pl.ds(0, SRC), :, pl.ds(d * CB, CB)], sem.at[d]))
    for group in range(2):
        copies.append(pltpu.make_async_copy(
            rows_in.at[:, pl.ds((base + 8 + group) * MAIN, MAIN)], left_ref.at[group], sem.at[8 + group]))
    return copies


def spread_rest(into, left_ref, picks):
    for d in range(8):
        left = left_ref[d // 4].reshape(FULL, CB)
        got = dot(picks[d % 4], left).astype(BF)
        into[SRC:ROWS // MAIN, :, d * CB:(d + 1) * CB] = got.reshape(ROWS // MAIN - SRC, MAIN, CB)


def main_kernel(rows_in, w_in, dgate_out, dup_out, gate_out, grad_out,
                x_ref, dy_ref, left_ref, w_ref, grad_ref, side_ref, pre_ref, gate_ref,
                x_sem, dy_sem, w_sem, out_sem, side_sem, gate_sem):
    x_copies = unpack(rows_in, 0, x_ref, left_ref.at[0], x_sem)
    dy_copies = unpack(rows_in, 10, dy_ref, left_ref.at[1], dy_sem)
    w_copies = [[[pltpu.make_async_copy(w_in.at[d, q, m], w_ref.at[q, m, d], w_sem.at[q, m, d])
                  for d in range(8)] for m in range(3)] for q in range(2)]
    batches = (
        x_copies + w_copies[0][0] + w_copies[0][1],
        w_copies[1][0] + w_copies[1][1],
        dy_copies + w_copies[0][2] + w_copies[1][2],
    )
    for batch in batches:
        for copy in batch:
            copy.start()
    picks = [rest_pick(k) for k in range(4)]
    outs = []
    for q in range(2):
        for copy in batches[q]:
            copy.wait()
        if q == 0:
            spread_rest(x_ref, left_ref.at[0], picks)
        x = x_ref[...].reshape(ROWS, D)
        pre_ref[q, 0] = dot(x, w_ref[q, 0].reshape(D, CB))
        pre_ref[q, 1] = dot(x, w_ref[q, 1].reshape(D, CB))
    for copy in batches[2]:
        copy.wait()
    spread_rest(dy_ref, left_ref.at[1], picks)
    for q in range(2):
        zeta = dot(dy_ref[...].reshape(ROWS, D), w_ref[q, 2].reshape(D, CB))
        gpre, upre = pre_ref[q, 0], pre_ref[q, 1]
        sig = jax.nn.sigmoid(gpre)
        act = gpre * sig
        hidden = (act * upre).astype(BF)
        side_ref[q, 2] = hidden
        part = jnp.sum(hidden.astype(F32) * zeta, axis=1, keepdims=True)
        part = jnp.broadcast_to(part, (ROWS, 128))
        gate_ref[...] = part if q == 0 else gate_ref[...] + part
        side_ref[q, 0] = (zeta * upre * sig * (1.0 + gpre * (1.0 - sig))).astype(BF)
        side_ref[q, 1] = (zeta * act).astype(BF)
        for d in range(8):
            for m, rows_ref in enumerate((x_ref, x_ref, dy_ref)):
                cols = rows_ref[:, :, d * CB:(d + 1) * CB].reshape(ROWS, CB)
                grad_ref[d, q, m] = dot(cols, side_ref[q, m], 0, 0).astype(BF)
            if d % 4 == 3:
                for done in range(d - 3, d + 1):
                    outs.append(pltpu.make_async_copy(
                        grad_ref.at[done, q], grad_out.at[done, q], out_sem.at[done, q]))
                    outs[-1].start()
            if d == 3:
                for m, out in enumerate((dgate_out, dup_out)):
                    outs.append(pltpu.make_async_copy(side_ref.at[q, m], out.at[q], side_sem.at[q, m]))
                    outs[-1].start()
    outs.append(pltpu.make_async_copy(gate_ref, gate_out, gate_sem.at[0]))
    outs[-1].start()
    for copy in outs:
        copy.wait()


def back_kernel(dgate_ref, dup_ref, gate_ref, w_in, out_ref, left_ref, w_ref, w_sem):
    copies = [pltpu.make_async_copy(w_in.at[:, q, m], w_ref.at[q, m], w_sem.at[q, m])
              for q in range(2) for m in range(2)]
    for copy in copies:
        copy.start()
    for copy in copies:
        copy.wait()
    picks = [rest_pick(k) for k in range(4)]
    for group in range(2):
        left = None
        for k in range(4):
            d = group * 4 + k
            total = dot(dgate_ref[0], w_ref[0, 0, d], 1, 1) + dot(dup_ref[0], w_ref[0, 1, d], 1, 1)
            total += dot(dgate_ref[1], w_ref[1, 0, d], 1, 1) + dot(dup_ref[1], w_ref[1, 1, d], 1, 1)
            rows = total.astype(BF)
            out_ref[:, d * MAIN:(d + 1) * MAIN, :] = rows[0:FULL].reshape(SRC, MAIN, CB)
            more = dot(picks[k], rows[FULL:ROWS], 0, 0)
            left = more if left is None else left + more
        at = (8 + group) * MAIN
        out_ref[:, at:at + MAIN, :] = left.astype(BF).reshape(SRC, MAIN, CB)
    gates = gate_ref[...].astype(BF)
    out_ref[:, 10 * MAIN:11 * MAIN, 0:128] = gates[0:FULL].reshape(SRC, MAIN, 128)
    spread = dot(picks[0], gates[FULL:ROWS], 0, 0).astype(BF)
    out_ref[:, 10 * MAIN:11 * MAIN, 128:256] = spread.reshape(SRC, MAIN, 128)


def finish_kernel(core_ref, kept_ref, came_ref, *out_refs):
    core = core_ref[0]
    for m, out_ref in enumerate(out_refs):
        out_ref[core] = kept_ref[0, m]
        out_ref[1 - core] = came_ref[1, m]


def combine_kernel(routes_ref, gates_ref, back_ref, grad_ref, gate_ref):
    first, second, slot = slots(routes_ref[...])
    gates = gates_ref[...].astype(F32)
    count = 2 * E * MAIN
    place = iota((128, count), 1)
    expand = (place // (4 * MAIN) * 2 + place // MAIN % 2 == iota((128, count), 0)).astype(F32).astype(BF)
    col = iota((T, count), 1)
    main_at = (col % MAIN).astype(F32)
    rest_at = (col % REST + MAIN).astype(F32)
    block = col // REST % 4
    slot_col = dot(slot.astype(BF), expand, 0, 0)
    main = (slot_col == main_at).astype(F32).astype(BF)
    rest = slot_col == rest_at
    rests = [jnp.logical_and(rest, block == k).astype(F32).astype(BF) for k in range(4)]
    for d in range(8):
        got = back_ref[:, d * MAIN:(d + 1) * MAIN, :].reshape(count, CB)
        at = (8 + d // 4) * MAIN
        more = back_ref[:, at:at + MAIN, :].reshape(count, CB)
        grad_ref[:, d * CB:(d + 1) * CB] = (dot(main, got) + dot(rests[d % 4], more)).astype(BF)
    parts = back_ref[:, 10 * MAIN:11 * MAIN, :].reshape(count, CB)
    for k, chosen in enumerate((first, second)):
        own = dot(jnp.where(chosen, slot, -1.0).astype(BF), expand, 0, 0)
        own = jnp.where(dot(chosen.astype(F32).astype(BF), expand, 0, 0) > 0.5, own, -1.0)
        a = (own == main_at).astype(F32).astype(BF)
        b = jnp.logical_and(own == rest_at, block == 0).astype(F32).astype(BF)
        value = dot(parts[:, 0:128], a, 0, 1) + dot(parts[:, 128:256], b, 0, 1)
        gate_ref[k:k + 1, :] = value[0:1, :] / gates[k:k + 1, :]


def vmem(count):
    return [pl.BlockSpec(memory_space=pltpu.VMEM)] * count


def params():
    return pltpu.CompilerParams(vmem_limit_bytes=60 * MB)


def cost(flops, moved):
    return pl.CostEstimate(flops=flops, bytes_accessed=moved, transcendentals=0)


def shape(*sizes, dtype=BF):
    return jax.ShapeDtypeStruct(sizes, dtype)


def call(kernel, name, outs, args, flops, moved, kinds=None, out_kinds=None, scratch=()):
    spaces = {"s": pltpu.SMEM, "v": pltpu.VMEM, "a": pl.ANY}
    kinds = kinds or "v" * len(args)
    out_kinds = out_kinds or "v" * len(outs)
    return pl.pallas_call(
        kernel,
        out_shape=tuple(outs),
        in_specs=[pl.BlockSpec(memory_space=spaces[k]) for k in kinds],
        out_specs=tuple(pl.BlockSpec(memory_space=spaces[k]) for k in out_kinds),
        scratch_shapes=list(scratch),
        compiler_params=params(),
        cost_estimate=cost(flops, moved),
        name=name,
    )(*args)


PARTNER = [(i, i ^ 1) for i in range(SRC)]


def per_device(inputs, cotangent, routes, gate_weights, gate_weight, up_weight, down_weight):
    core = (lax.axis_index("eslice") % 2).reshape(1)
    dma = pltpu.SemaphoreType.DMA
    mats = (gate_weight, up_weight, down_weight)

    theirs = [lax.ppermute(w, "eslice", PARTNER) for w in mats]
    (packed,) = call(pack_kernel, "pack", [shape(2, 3, CB, CB)], (core, *mats, *theirs), 0, 2 * MB,
                     kinds="svvvvvv")
    weights = lax.all_gather(packed, "dp", axis=0, tiled=False)

    (sent,) = call(send_kernel, "send", [shape(E // 2, 2, 2, 20 * MAIN, CB)],
                   (routes.T, gate_weights.T, inputs, cotangent), 10**9, 6 * MB)
    rows = lax.all_to_all(sent.reshape(SRC, 20 * MAIN, CB), "eslice", 0, 0, tiled=True)

    tiles = pltpu.VMEM((ROWS // MAIN, MAIN, D), BF)
    dgate, dup, gate_part, grads = call(
        main_kernel, "main",
        [shape(2, ROWS, CB), shape(2, ROWS, CB), shape(ROWS, 128, dtype=F32), shape(8, 2, 3, CB, CB)],
        (rows, weights), 8 * 10**9, 24 * MB, kinds="aa", out_kinds="aaaa",
        scratch=(tiles, tiles, pltpu.VMEM((2, 2, SRC, MAIN, CB), BF), pltpu.VMEM((2, 3, 8, CB, CB), BF),
                 pltpu.VMEM((8, 2, 3, CB, CB), BF), pltpu.VMEM((2, 3, ROWS, CB), BF),
                 pltpu.VMEM((2, 2, ROWS, CB), F32), pltpu.VMEM((ROWS, 128), F32),
                 dma((10,)), dma((10,)), dma((2, 3, 8)), dma((8, 2)), dma((2, 2)), dma((1,))))
    reduced = lax.psum_scatter(grads, "dp", scatter_dimension=0, tiled=False)

    (back,) = call(
        back_kernel, "back", [shape(SRC, 11 * MAIN, CB)], (dgate, dup, gate_part, weights),
        3 * 10**9, 12 * MB, kinds="vvva",
        scratch=(pltpu.VMEM((2, FULL, CB), F32), pltpu.VMEM((2, 2, 8, CB, CB), BF), dma((2, 2))))
    returned = lax.all_to_all(back, "eslice", 0, 0, tiled=True)
    input_grad, gate_grad = call(combine_kernel, "combine", [shape(T, D), shape(2, T, dtype=F32)],
                                 (routes.T, gate_weights.T, returned), 10**9, 4 * MB)

    reduced, input_grad = lax.optimization_barrier((reduced, input_grad))
    came = lax.ppermute(reduced, "eslice", PARTNER)
    grads = call(finish_kernel, "finish", [shape(2, CB, CB)] * 3,
                 (core, reduced, came), 10**6, 3 * MB, kinds="svv")
    return (input_grad, gate_grad.T, *grads)


def solution(mesh):
    token = P(("dp", "eslice"), None)
    weight = P("eslice", "dp", None)
    return jax.shard_map(
        per_device,
        mesh=mesh,
        in_specs=(token,) * 4 + (weight,) * 3,
        out_specs=(token,) * 2 + (weight,) * 3,
        check_vma=False,
    )
```

```python
import functools

import jax
import jax.numpy as jnp
from jax import lax
from jax.experimental import pallas as pl
from jax.experimental.pallas import tpu as pltpu
from jax.sharding import PartitionSpec as P

BF = jnp.bfloat16
F32 = jnp.float32
T = 128
D = 2048
E = 16
SRC = 32
MAIN = 16
REST = 4
ROWS = SRC * (MAIN + REST)
FULL = SRC * MAIN
CB = 256
MB = 1 << 20


def iota(shape, dim):
    return lax.broadcasted_iota(jnp.int32, shape, dim)


def dot(a, b, ca=1, cb=0):
    return lax.dot_general(a, b, (((ca,), (cb,)), ((), ())), preferred_element_type=F32)


def slots(routes):
    expert = iota((128, T), 0)
    first = routes[0:1, :] == expert
    second = routes[1:2, :] == expert
    member = jnp.logical_or(first, second)
    before = (iota((T, T), 0) < iota((T, T), 1)).astype(F32).astype(BF)
    position = dot(member.astype(F32).astype(BF), before)
    return first, second, jnp.where(member, position, -1.0)


def send_kernel(routes_ref, gates_ref, x_ref, dy_ref, out_ref, made_ref, sem):
    first, second, slot = slots(routes_ref[...])
    gates = gates_ref[...].astype(F32)
    gate = jnp.where(first, gates[0:1, :], 0.0) + jnp.where(second, gates[1:2, :], 0.0)
    count = E * MAIN
    expand = (iota((count, 128), 0) // MAIN == iota((count, 128), 1)).astype(F32).astype(BF)
    slot_row = dot(expand, slot.astype(BF))
    gate_row = dot(expand, gate.astype(BF))
    row = iota((count, T), 0)
    main = slot_row == (row % MAIN).astype(F32)
    rest = slot_row == (row % REST + MAIN).astype(F32)
    block = row // REST % 4

    outs = []
    for which, (values, src_ref) in enumerate(((1.0, x_ref), (gate_row, dy_ref))):
        pick = jnp.where(main, values, 0.0).astype(BF)
        picks = [jnp.where(jnp.logical_and(rest, block == k), values, 0.0).astype(BF) for k in range(4)]
        made = made_ref.at[which]

        def put(at, rows):
            made[:, :, at * MAIN:(at + 1) * MAIN, :] = rows.astype(BF).reshape(E // 2, 2, MAIN, CB)

        for group in range(2):
            left = None
            for k in range(4):
                d = group * 4 + k
                cols = src_ref[:, d * CB:(d + 1) * CB]
                put(d, dot(pick, cols))
                more = dot(picks[k], cols)
                left = more if left is None else left + more
            put(8 + group, left)
        for side in range(2):
            place = out_ref.at[:, side, :, pl.ds(which * 10 * MAIN, 10 * MAIN), :]
            outs.append(pltpu.make_async_copy(made, place, sem.at[which, side]))
            outs[-1].start()
    for copy in outs:
        copy.wait()


def rest_pick(k):
    shape = (SRC * REST, FULL)
    r, c = iota(shape, 0), iota(shape, 1)
    hit = jnp.logical_and(r // REST == c // MAIN, r % REST == c % REST)
    return jnp.logical_and(hit, c // REST % 4 == k).astype(F32).astype(BF)


def pack_kernel(core_ref, *refs):
    ins, out_ref, held, in_sem, out_sem = refs[:6], *refs[6:]
    copies = [(pltpu.make_async_copy(ref.at[core_ref[0]], held.at[i // 3, i % 3], in_sem.at[i]),
               pltpu.make_async_copy(held.at[i // 3, i % 3], out_ref.at[i // 3, i % 3], out_sem.at[i]))
              for i, ref in enumerate(ins)]
    for fetch, _ in copies:
        fetch.start()
    for fetch, place in copies:
        fetch.wait()
        place.start()
    for _, place in copies:
        place.wait()


def unpack(rows_in, base, into, left_ref, sem):
    copies = []
    for d in range(8):
        copies.append(pltpu.make_async_copy(
            rows_in.at[:, pl.ds((base + d) * MAIN, MAIN)],
            into.at[pl.ds(0, SRC), :, pl.ds(d * CB, CB)], sem.at[d]))
    for group in range(2):
        copies.append(pltpu.make_async_copy(
            rows_in.at[:, pl.ds((base + 8 + group) * MAIN, MAIN)], left_ref.at[group], sem.at[8 + group]))
    return copies


def spread_rest(into, left_ref, picks):
    for d in range(8):
        left = left_ref[d // 4].reshape(FULL, CB)
        got = dot(picks[d % 4], left).astype(BF)
        into[SRC:ROWS // MAIN, :, d * CB:(d + 1) * CB] = got.reshape(ROWS // MAIN - SRC, MAIN, CB)


def grad_block(rows_ref, side_ref, cols):
    return dot(rows_ref[:, :, cols].reshape(ROWS, CB), side_ref[...], 0, 0).astype(BF)


def main_kernel(rows_in, w_in, side_out, gate_out, grad_out,
                x_ref, dy_ref, left_ref, w_ref, grad_ref, side_ref, pre_ref, gate_ref,
                x_sem, dy_sem, w_sem, out_sem, end_sem):
    x_copies = unpack(rows_in, 0, x_ref, left_ref.at[0], x_sem)
    dy_copies = unpack(rows_in, 10, dy_ref, left_ref.at[1], dy_sem)
    w_copies = [[[pltpu.make_async_copy(w_in.at[d, q, m], w_ref.at[q, m, d], w_sem.at[q, m, d])
                  for d in range(8)] for m in range(3)] for q in range(2)]
    batches = (
        x_copies + w_copies[0][0] + w_copies[0][1],
        w_copies[1][0] + w_copies[1][1],
        dy_copies + w_copies[0][2] + w_copies[1][2],
    )
    for batch in batches:
        for copy in batch:
            copy.start()
    picks = [rest_pick(k) for k in range(4)]
    for q in range(2):
        for copy in batches[q]:
            copy.wait()
        if q == 0:
            spread_rest(x_ref, left_ref.at[0], picks)
        x = x_ref[...].reshape(ROWS, D)
        pre_ref[q, 0] = dot(x, w_ref[q, 0].reshape(D, CB))
        pre_ref[q, 1] = dot(x, w_ref[q, 1].reshape(D, CB))
    for copy in batches[2]:
        copy.wait()
    spread_rest(dy_ref, left_ref.at[1], picks)
    for q in range(2):
        zeta = dot(dy_ref[...].reshape(ROWS, D), w_ref[q, 2].reshape(D, CB))
        gpre, upre = pre_ref[q, 0], pre_ref[q, 1]
        sig = jax.nn.sigmoid(gpre)
        act = gpre * sig
        hidden = (act * upre).astype(BF)
        part = jnp.sum(hidden.astype(F32) * zeta, axis=1, keepdims=True)
        part = jnp.broadcast_to(part, (ROWS, 128))
        gate_ref[...] = part if q == 0 else gate_ref[...] + part
        side_ref[q, 0] = (zeta * upre * sig * (1.0 + gpre * (1.0 - sig))).astype(BF)
        side_ref[q, 1] = (zeta * act).astype(BF)
        side_ref[q, 2] = hidden
    rows_refs = (x_ref, x_ref, dy_ref)
    outs = [pltpu.make_async_copy(gate_ref, gate_out, end_sem.at[0]),
            pltpu.make_async_copy(side_ref.at[:, pl.ds(0, 2)], side_out, end_sem.at[1])]
    for d in range(8):
        cols = slice(d * CB, (d + 1) * CB)
        for q in range(2):
            for m in range(3):
                grad_ref[d, q, m] = grad_block(rows_refs[m], side_ref.at[q, m], cols)
        outs.append(pltpu.make_async_copy(grad_ref.at[d], grad_out.at[d], out_sem.at[d]))
        if d % 2 == 1:
            for copy in outs[-2:] if d > 1 else outs:
                copy.start()
    for copy in outs:
        copy.wait()


def back_kernel(w_in, side_in, gate_in, back_out, w_ref, side_ref, gate_ref, back_ref, w_sem, end_sem):
    first = [pltpu.make_async_copy(side_in, side_ref, end_sem.at[0]),
             pltpu.make_async_copy(gate_in, gate_ref, end_sem.at[1])]
    w_copies = [[pltpu.make_async_copy(w_in.at[d, q, m], w_ref.at[q, m, d], w_sem.at[q, m, d])
                 for q in range(2) for m in range(2)] for d in range(8)]
    for copy in first + [copy for copies in w_copies for copy in copies]:
        copy.start()
    picks = [rest_pick(k) for k in range(4)]
    for copy in first:
        copy.wait()
    outs = []

    def put(at):
        rows = (slice(None), pl.ds(at * MAIN, MAIN))
        outs.append(pltpu.make_async_copy(back_ref.at[rows], back_out.at[rows], end_sem.at[2 + at]))
        outs[-1].start()

    gates = gate_ref[...].astype(BF)
    back_ref[:, 10 * MAIN:11 * MAIN, 0:128] = gates[0:FULL].reshape(SRC, MAIN, 128)
    spread = dot(picks[0], gates[FULL:ROWS], 0, 0).astype(BF)
    back_ref[:, 10 * MAIN:11 * MAIN, 128:256] = spread.reshape(SRC, MAIN, 128)
    put(10)
    for group in range(2):
        left = None
        for copies in w_copies[group * 4:group * 4 + 4]:
            for copy in copies:
                copy.wait()
        for k in range(4):
            d = group * 4 + k
            total = dot(side_ref[0, 0], w_ref[0, 0, d], 1, 1) + dot(side_ref[0, 1], w_ref[0, 1, d], 1, 1)
            total += dot(side_ref[1, 0], w_ref[1, 0, d], 1, 1) + dot(side_ref[1, 1], w_ref[1, 1, d], 1, 1)
            rows = total.astype(BF)
            back_ref[:, d * MAIN:(d + 1) * MAIN, :] = rows[0:FULL].reshape(SRC, MAIN, CB)
            more = dot(picks[k], rows[FULL:ROWS], 0, 0)
            left = more if left is None else left + more
        back_ref[:, (8 + group) * MAIN:(9 + group) * MAIN, :] = left.astype(BF).reshape(SRC, MAIN, CB)
        for at in (*range(group * 4, group * 4 + 4), 8 + group):
            put(at)
    for copy in outs:
        copy.wait()


def finish_kernel(core_ref, own_ref, came_ref, *refs):
    outs, (held, in_sem, out_sem) = refs[:3], refs[3:]
    core = core_ref[0]
    fetches = [pltpu.make_async_copy(own_ref.at[0, m], held.at[m], in_sem.at[m]) for m in range(3)]
    places = [pltpu.make_async_copy(held.at[m], outs[m].at[core], out_sem.at[m]) for m in range(3)]
    came = [pltpu.make_async_copy(came_ref.at[1, m], outs[m].at[1 - core], out_sem.at[3 + m]) for m in range(3)]
    for copy in fetches + came:
        copy.start()
    for fetch, place in zip(fetches, places):
        fetch.wait()
        place.start()
    for copy in came + places:
        copy.wait()


def combine_kernel(routes_ref, gates_ref, back_ref, grad_ref, gate_ref):
    first, second, slot = slots(routes_ref[...])
    gates = gates_ref[...].astype(F32)
    count = 2 * E * MAIN
    place = iota((128, count), 1)
    expand = (place // (4 * MAIN) * 2 + place // MAIN % 2 == iota((128, count), 0)).astype(F32).astype(BF)
    col = iota((T, count), 1)
    main_at = (col % MAIN).astype(F32)
    rest_at = (col % REST + MAIN).astype(F32)
    block = col // REST % 4
    slot_col = dot(slot.astype(BF), expand, 0, 0)
    main = (slot_col == main_at).astype(F32).astype(BF)
    rest = slot_col == rest_at
    rests = [jnp.logical_and(rest, block == k).astype(F32).astype(BF) for k in range(4)]
    for d in range(8):
        got = back_ref[:, d * MAIN:(d + 1) * MAIN, :].reshape(count, CB)
        at = (8 + d // 4) * MAIN
        more = back_ref[:, at:at + MAIN, :].reshape(count, CB)
        grad_ref[:, d * CB:(d + 1) * CB] = (dot(main, got) + dot(rests[d % 4], more)).astype(BF)
    parts = back_ref[:, 10 * MAIN:11 * MAIN, :].reshape(count, CB)
    for k, chosen in enumerate((first, second)):
        own = dot(jnp.where(chosen, slot, -1.0).astype(BF), expand, 0, 0)
        own = jnp.where(dot(chosen.astype(F32).astype(BF), expand, 0, 0) > 0.5, own, -1.0)
        a = (own == main_at).astype(F32).astype(BF)
        b = jnp.logical_and(own == rest_at, block == 0).astype(F32).astype(BF)
        value = dot(parts[:, 0:128], a, 0, 1) + dot(parts[:, 128:256], b, 0, 1)
        gate_ref[k:k + 1, :] = value[0:1, :] / gates[k:k + 1, :]


def vmem(count):
    return [pl.BlockSpec(memory_space=pltpu.VMEM)] * count


def cost(flops, moved):
    return pl.CostEstimate(flops=flops, bytes_accessed=moved, transcendentals=0)


def shape(*sizes, dtype=BF):
    return jax.ShapeDtypeStruct(sizes, dtype)


def call(kernel, name, outs, args, flops, moved, kinds=None, out_kinds=None, scratch=(), limit=63400000):
    spaces = {"s": pltpu.SMEM, "v": pltpu.VMEM, "a": pl.ANY}
    kinds = kinds or "v" * len(args)
    out_kinds = out_kinds or "v" * len(outs)
    return pl.pallas_call(
        kernel,
        out_shape=tuple(outs),
        in_specs=[pl.BlockSpec(memory_space=spaces[k]) for k in kinds],
        out_specs=tuple(pl.BlockSpec(memory_space=spaces[k]) for k in out_kinds),
        scratch_shapes=list(scratch),
        compiler_params=pltpu.CompilerParams(vmem_limit_bytes=limit),
        cost_estimate=cost(flops, moved),
        name=name,
    )(*args)


PARTNER = [(i, i ^ 1) for i in range(SRC)]


def per_device(inputs, cotangent, routes, gate_weights, gate_weight, up_weight, down_weight):
    core = (lax.axis_index("eslice") % 2).reshape(1)
    dma = pltpu.SemaphoreType.DMA
    mats = (gate_weight, up_weight, down_weight)

    theirs = [lax.ppermute(w, "eslice", PARTNER) for w in mats]
    (packed,) = call(pack_kernel, "pack", [shape(2, 3, CB, CB)], (core, *mats, *theirs), 0, 2 * MB,
                     kinds="saaaaaa", out_kinds="a",
                     scratch=(pltpu.VMEM((2, 3, CB, CB), BF), dma((6,)), dma((6,))))
    weights = lax.all_gather(packed, "dp", axis=0, tiled=False)

    (sent,) = call(send_kernel, "send", [shape(E // 2, 2, 2, 20 * MAIN, CB)],
                   (routes.T, gate_weights.T, inputs, cotangent), 10**9, 6 * MB, kinds="vvvv", out_kinds="a",
                   scratch=(pltpu.VMEM((2, E // 2, 2, 10 * MAIN, CB), BF), dma((2, 2))))
    rows = lax.all_to_all(sent.reshape(SRC, 20 * MAIN, CB), "eslice", 0, 0, tiled=True)

    tiles = pltpu.VMEM((ROWS // MAIN, MAIN, D), BF)
    rests = pltpu.VMEM((2, 2, SRC, MAIN, CB), BF)
    gate_vmem = pltpu.VMEM((ROWS, 128), F32)
    side, gate_part, grads = call(
        main_kernel, "main",
        [shape(2, 2, ROWS, CB), shape(ROWS, 128, dtype=F32), shape(8, 2, 3, CB, CB)],
        (rows, weights), 8 * 10**9, 24 * MB, kinds="aa", out_kinds="aaa",
        scratch=(tiles, tiles, rests, pltpu.VMEM((2, 3, 8, CB, CB), BF),
                 pltpu.VMEM((8, 2, 3, CB, CB), BF), pltpu.VMEM((2, 3, ROWS, CB), BF),
                 pltpu.VMEM((2, 2, ROWS, CB), F32), gate_vmem,
                 dma((10,)), dma((10,)), dma((2, 3, 8)), dma((8,)), dma((2,))))
    reduced = lax.psum_scatter(grads, "dp", scatter_dimension=0, tiled=False)

    (back,) = call(
        back_kernel, "back", [shape(SRC, 11 * MAIN, CB)], (weights, side, gate_part), 3 * 10**9, 10 * MB,
        kinds="aaa", out_kinds="a",
        scratch=(pltpu.VMEM((2, 2, 8, CB, CB), BF), pltpu.VMEM((2, 2, ROWS, CB), BF), gate_vmem,
                 pltpu.VMEM((SRC, 11 * MAIN, CB), BF), dma((2, 2, 8)), dma((13,))))
    returned = lax.all_to_all(back, "eslice", 0, 0, tiled=True)
    input_grad, gate_grad = call(combine_kernel, "combine", [shape(T, D), shape(2, T, dtype=F32)],
                                 (routes.T, gate_weights.T, returned), 10**9, 4 * MB)
    reduced, input_grad = lax.optimization_barrier((reduced, input_grad))
    came = lax.ppermute(reduced, "eslice", PARTNER)
    grads = call(finish_kernel, "finish", [shape(2, CB, CB)] * 3, (core, reduced, came), 10**6, 3 * MB,
                 kinds="sav", out_kinds="aaa", limit=4 * MB,
                 scratch=(pltpu.VMEM((3, CB, CB), BF), dma((3,)), dma((6,))))
    return (input_grad, gate_grad.T, *grads)


def solution(mesh):
    token = P(("dp", "eslice"), None)
    weight = P("eslice", "dp", None)
    return jax.shard_map(
        per_device,
        mesh=mesh,
        in_specs=(token,) * 4 + (weight,) * 3,
        out_specs=(token,) * 2 + (weight,) * 3,
        check_vma=False,
    )
```

```python
import functools

import jax
import jax.numpy as jnp
from jax import lax
from jax.experimental import pallas as pl
from jax.experimental.pallas import tpu as pltpu
from jax.sharding import PartitionSpec as P

BF = jnp.bfloat16
F32 = jnp.float32
T = 128
D = 2048
E = 16
SRC = 32
MAIN = 16
REST = 4
ROWS = SRC * (MAIN + REST)
FULL = SRC * MAIN
CB = 256
MB = 1 << 20


def iota(shape, dim):
    return lax.broadcasted_iota(jnp.int32, shape, dim)


def dot(a, b, ca=1, cb=0):
    return lax.dot_general(a, b, (((ca,), (cb,)), ((), ())), preferred_element_type=F32)


def slots(routes):
    expert = iota((128, T), 0)
    first = routes[0:1, :] == expert
    second = routes[1:2, :] == expert
    member = jnp.logical_or(first, second)
    before = (iota((T, T), 0) < iota((T, T), 1)).astype(F32).astype(BF)
    position = dot(member.astype(F32).astype(BF), before)
    return first, second, jnp.where(member, position, -1.0)


def send_kernel(routes_ref, gates_ref, x_ref, dy_ref, out_ref, made_ref, sem):
    first, second, slot = slots(routes_ref[...])
    gates = gates_ref[...].astype(F32)
    gate = jnp.where(first, gates[0:1, :], 0.0) + jnp.where(second, gates[1:2, :], 0.0)
    count = E * MAIN
    expand = (iota((count, 128), 0) // MAIN == iota((count, 128), 1)).astype(F32).astype(BF)
    slot_row = dot(expand, slot.astype(BF))
    gate_row = dot(expand, gate.astype(BF))
    row = iota((count, T), 0)
    main = slot_row == (row % MAIN).astype(F32)
    rest = slot_row == (row % REST + MAIN).astype(F32)
    block = row // REST % 4

    outs = []
    for which, (values, src_ref) in enumerate(((1.0, x_ref), (gate_row, dy_ref))):
        pick = jnp.where(main, values, 0.0).astype(BF)
        picks = [jnp.where(jnp.logical_and(rest, block == k), values, 0.0).astype(BF) for k in range(4)]
        made = made_ref.at[which]

        def put(at, rows):
            made[:, :, at * MAIN:(at + 1) * MAIN, :] = rows.astype(BF).reshape(E // 2, 2, MAIN, CB)

        for group in range(2):
            left = None
            for k in range(4):
                d = group * 4 + k
                cols = src_ref[:, d * CB:(d + 1) * CB]
                put(d, dot(pick, cols))
                more = dot(picks[k], cols)
                left = more if left is None else left + more
            put(8 + group, left)
        for side in range(2):
            place = out_ref.at[:, side, :, pl.ds(which * 10 * MAIN, 10 * MAIN), :]
            outs.append(pltpu.make_async_copy(made, place, sem.at[which, side]))
            outs[-1].start()
    for copy in outs:
        copy.wait()


def rest_pick(k):
    shape = (SRC * REST, FULL)
    r, c = iota(shape, 0), iota(shape, 1)
    hit = jnp.logical_and(r // REST == c // MAIN, r % REST == c % REST)
    return jnp.logical_and(hit, c // REST % 4 == k).astype(F32).astype(BF)


def unpack(rows_in, base, into, left_ref, sem):
    copies = []
    for d in range(8):
        copies.append(pltpu.make_async_copy(
            rows_in.at[:, pl.ds((base + d) * MAIN, MAIN)],
            into.at[pl.ds(0, SRC), :, pl.ds(d * CB, CB)], sem.at[d]))
    for group in range(2):
        copies.append(pltpu.make_async_copy(
            rows_in.at[:, pl.ds((base + 8 + group) * MAIN, MAIN)], left_ref.at[group], sem.at[8 + group]))
    return copies


def spread_rest(into, left_ref, picks):
    for d in range(8):
        left = left_ref[d // 4].reshape(FULL, CB)
        got = dot(picks[d % 4], left).astype(BF)
        into[SRC:ROWS // MAIN, :, d * CB:(d + 1) * CB] = got.reshape(ROWS // MAIN - SRC, MAIN, CB)


def grad_block(rows_ref, side_ref, cols):
    return dot(rows_ref[:, :, cols].reshape(ROWS, CB), side_ref[...], 0, 0).astype(BF)


def main_kernel(rows_in, w_in, side_out, gate_out, grad_out,
                x_ref, dy_ref, left_ref, w_ref, grad_ref, side_ref, pre_ref, gate_ref,
                x_sem, dy_sem, w_sem, out_sem, end_sem):
    x_copies = unpack(rows_in, 0, x_ref, left_ref.at[0], x_sem)
    dy_copies = unpack(rows_in, 10, dy_ref, left_ref.at[1], dy_sem)
    w_copies = [[[pltpu.make_async_copy(w_in.at[d, q, m], w_ref.at[q, m, d], w_sem.at[q, m, d])
                  for d in range(8)] for m in range(3)] for q in range(2)]
    batches = (
        x_copies + w_copies[0][0] + w_copies[0][1],
        w_copies[1][0] + w_copies[1][1],
        dy_copies + w_copies[0][2] + w_copies[1][2],
    )
    for batch in batches:
        for copy in batch:
            copy.start()
    picks = [rest_pick(k) for k in range(4)]
    for q in range(2):
        for copy in batches[q]:
            copy.wait()
        if q == 0:
            spread_rest(x_ref, left_ref.at[0], picks)
        x = x_ref[...].reshape(ROWS, D)
        pre_ref[q, 0] = dot(x, w_ref[q, 0].reshape(D, CB))
        pre_ref[q, 1] = dot(x, w_ref[q, 1].reshape(D, CB))
    for copy in batches[2]:
        copy.wait()
    spread_rest(dy_ref, left_ref.at[1], picks)
    for q in range(2):
        zeta = dot(dy_ref[...].reshape(ROWS, D), w_ref[q, 2].reshape(D, CB))
        gpre, upre = pre_ref[q, 0], pre_ref[q, 1]
        sig = jax.nn.sigmoid(gpre)
        act = gpre * sig
        hidden = (act * upre).astype(BF)
        part = jnp.sum(hidden.astype(F32) * zeta, axis=1, keepdims=True)
        part = jnp.broadcast_to(part, (ROWS, 128))
        gate_ref[...] = part if q == 0 else gate_ref[...] + part
        side_ref[q, 0] = (zeta * upre * sig * (1.0 + gpre * (1.0 - sig))).astype(BF)
        side_ref[q, 1] = (zeta * act).astype(BF)
        side_ref[q, 2] = hidden
    rows_refs = (x_ref, x_ref, dy_ref)
    outs = [pltpu.make_async_copy(gate_ref, gate_out, end_sem.at[0]),
            pltpu.make_async_copy(side_ref.at[:, pl.ds(0, 2)], side_out, end_sem.at[1])]
    for d in range(8):
        cols = slice(d * CB, (d + 1) * CB)
        for q in range(2):
            for m in range(3):
                grad_ref[d, q, m] = grad_block(rows_refs[m], side_ref.at[q, m], cols)
        outs.append(pltpu.make_async_copy(grad_ref.at[d], grad_out.at[d], out_sem.at[d]))
        if d % 2 == 1:
            for copy in outs[-2:] if d > 1 else outs:
                copy.start()
    for copy in outs:
        copy.wait()


def back_kernel(w_in, side_in, gate_in, back_out, w_ref, side_ref, gate_ref, back_ref, w_sem, end_sem):
    first = [pltpu.make_async_copy(side_in, side_ref, end_sem.at[0]),
             pltpu.make_async_copy(gate_in, gate_ref, end_sem.at[1])]
    w_copies = [[pltpu.make_async_copy(w_in.at[d, q, m], w_ref.at[q, m, d], w_sem.at[q, m, d])
                 for q in range(2) for m in range(2)] for d in range(8)]
    for copy in first + [copy for copies in w_copies for copy in copies]:
        copy.start()
    picks = [rest_pick(k) for k in range(4)]
    for copy in first:
        copy.wait()
    outs = []

    def put(at):
        rows = (slice(None), pl.ds(at * MAIN, MAIN))
        outs.append(pltpu.make_async_copy(back_ref.at[rows], back_out.at[rows], end_sem.at[2 + at]))
        outs[-1].start()

    gates = gate_ref[...].astype(BF)
    back_ref[:, 10 * MAIN:11 * MAIN, 0:128] = gates[0:FULL].reshape(SRC, MAIN, 128)
    spread = dot(picks[0], gates[FULL:ROWS], 0, 0).astype(BF)
    back_ref[:, 10 * MAIN:11 * MAIN, 128:256] = spread.reshape(SRC, MAIN, 128)
    put(10)
    for group in range(2):
        left = None
        for copies in w_copies[group * 4:group * 4 + 4]:
            for copy in copies:
                copy.wait()
        for k in range(4):
            d = group * 4 + k
            total = dot(side_ref[0, 0], w_ref[0, 0, d], 1, 1) + dot(side_ref[0, 1], w_ref[0, 1, d], 1, 1)
            total += dot(side_ref[1, 0], w_ref[1, 0, d], 1, 1) + dot(side_ref[1, 1], w_ref[1, 1, d], 1, 1)
            rows = total.astype(BF)
            back_ref[:, d * MAIN:(d + 1) * MAIN, :] = rows[0:FULL].reshape(SRC, MAIN, CB)
            more = dot(picks[k], rows[FULL:ROWS], 0, 0)
            left = more if left is None else left + more
        back_ref[:, (8 + group) * MAIN:(9 + group) * MAIN, :] = left.astype(BF).reshape(SRC, MAIN, CB)
        for at in (*range(group * 4, group * 4 + 4), 8 + group):
            put(at)
    for copy in outs:
        copy.wait()


def combine_kernel(routes_ref, gates_ref, back_ref, grad_ref, gate_ref):
    first, second, slot = slots(routes_ref[...])
    gates = gates_ref[...].astype(F32)
    count = 2 * E * MAIN
    place = iota((128, count), 1)
    expand = (place // (4 * MAIN) * 2 + place // MAIN % 2 == iota((128, count), 0)).astype(F32).astype(BF)
    col = iota((T, count), 1)
    main_at = (col % MAIN).astype(F32)
    rest_at = (col % REST + MAIN).astype(F32)
    block = col // REST % 4
    slot_col = dot(slot.astype(BF), expand, 0, 0)
    main = (slot_col == main_at).astype(F32).astype(BF)
    rest = slot_col == rest_at
    rests = [jnp.logical_and(rest, block == k).astype(F32).astype(BF) for k in range(4)]
    for d in range(8):
        got = back_ref[:, d * MAIN:(d + 1) * MAIN, :].reshape(count, CB)
        at = (8 + d // 4) * MAIN
        more = back_ref[:, at:at + MAIN, :].reshape(count, CB)
        grad_ref[:, d * CB:(d + 1) * CB] = (dot(main, got) + dot(rests[d % 4], more)).astype(BF)
    parts = back_ref[:, 10 * MAIN:11 * MAIN, :].reshape(count, CB)
    for k, chosen in enumerate((first, second)):
        own = dot(jnp.where(chosen, slot, -1.0).astype(BF), expand, 0, 0)
        own = jnp.where(dot(chosen.astype(F32).astype(BF), expand, 0, 0) > 0.5, own, -1.0)
        a = (own == main_at).astype(F32).astype(BF)
        b = jnp.logical_and(own == rest_at, block == 0).astype(F32).astype(BF)
        value = dot(parts[:, 0:128], a, 0, 1) + dot(parts[:, 128:256], b, 0, 1)
        gate_ref[k:k + 1, :] = value[0:1, :] / gates[k:k + 1, :]


def vmem(count):
    return [pl.BlockSpec(memory_space=pltpu.VMEM)] * count


def cost(flops, moved):
    return pl.CostEstimate(flops=flops, bytes_accessed=moved, transcendentals=0)


def shape(*sizes, dtype=BF):
    return jax.ShapeDtypeStruct(sizes, dtype)


def call(kernel, name, outs, args, flops, moved, kinds=None, out_kinds=None, scratch=(), limit=63400000):
    spaces = {"s": pltpu.SMEM, "v": pltpu.VMEM, "a": pl.ANY}
    kinds = kinds or "v" * len(args)
    out_kinds = out_kinds or "v" * len(outs)
    return pl.pallas_call(
        kernel,
        out_shape=tuple(outs),
        in_specs=[pl.BlockSpec(memory_space=spaces[k]) for k in kinds],
        out_specs=tuple(pl.BlockSpec(memory_space=spaces[k]) for k in out_kinds),
        scratch_shapes=list(scratch),
        compiler_params=pltpu.CompilerParams(vmem_limit_bytes=limit),
        cost_estimate=cost(flops, moved),
        name=name,
    )(*args)


PARTNER = [(i, i ^ 1) for i in range(SRC)]


def per_device(inputs, cotangent, routes, gate_weights, gate_weight, up_weight, down_weight):
    core = lax.axis_index("eslice") % 2
    dma = pltpu.SemaphoreType.DMA
    mats = (gate_weight, up_weight, down_weight)

    theirs = [lax.ppermute(w, "eslice", PARTNER) for w in mats]
    second = core == 1
    packed = jnp.stack([jnp.where(second, w[1], w[0]) for w in (*mats, *theirs)]).reshape(2, 3, CB, CB)
    weights = lax.all_gather(packed, "dp", axis=0, tiled=False)

    (sent,) = call(send_kernel, "send", [shape(E // 2, 2, 2, 20 * MAIN, CB)],
                   (routes.T, gate_weights.T, inputs, cotangent), 10**9, 6 * MB, kinds="vvvv", out_kinds="a",
                   scratch=(pltpu.VMEM((2, E // 2, 2, 10 * MAIN, CB), BF), dma((2, 2))))
    rows = lax.all_to_all(sent.reshape(SRC, 20 * MAIN, CB), "eslice", 0, 0, tiled=True)

    tiles = pltpu.VMEM((ROWS // MAIN, MAIN, D), BF)
    rests = pltpu.VMEM((2, 2, SRC, MAIN, CB), BF)
    gate_vmem = pltpu.VMEM((ROWS, 128), F32)
    side, gate_part, grads = call(
        main_kernel, "main",
        [shape(2, 2, ROWS, CB), shape(ROWS, 128, dtype=F32), shape(8, 2, 3, CB, CB)],
        (rows, weights), 8 * 10**9, 24 * MB, kinds="aa", out_kinds="aaa",
        scratch=(tiles, tiles, rests, pltpu.VMEM((2, 3, 8, CB, CB), BF),
                 pltpu.VMEM((8, 2, 3, CB, CB), BF), pltpu.VMEM((2, 3, ROWS, CB), BF),
                 pltpu.VMEM((2, 2, ROWS, CB), F32), gate_vmem,
                 dma((10,)), dma((10,)), dma((2, 3, 8)), dma((8,)), dma((2,))))
    reduced = lax.psum_scatter(grads, "dp", scatter_dimension=0, tiled=False)

    (back,) = call(
        back_kernel, "back", [shape(SRC, 11 * MAIN, CB)], (weights, side, gate_part), 3 * 10**9, 10 * MB,
        kinds="aaa", out_kinds="a",
        scratch=(pltpu.VMEM((2, 2, 8, CB, CB), BF), pltpu.VMEM((2, 2, ROWS, CB), BF), gate_vmem,
                 pltpu.VMEM((SRC, 11 * MAIN, CB), BF), dma((2, 2, 8)), dma((13,))))
    returned = lax.all_to_all(back, "eslice", 0, 0, tiled=True)
    input_grad, gate_grad = call(combine_kernel, "combine", [shape(T, D), shape(2, T, dtype=F32)],
                                 (routes.T, gate_weights.T, returned), 10**9, 4 * MB)
    reduced, input_grad = lax.optimization_barrier((reduced, input_grad))
    came = lax.ppermute(reduced, "eslice", PARTNER)
    grads = []
    for m in range(3):
        low, high = (jnp.where(first, reduced[0, m], came[1, m]) for first in (core == 0, second))
        grads.append(jnp.stack((low, high)))
    return (input_grad, gate_grad.T, *grads)


def solution(mesh):
    token = P(("dp", "eslice"), None)
    weight = P("eslice", "dp", None)
    return jax.shard_map(
        per_device,
        mesh=mesh,
        in_specs=(token,) * 4 + (weight,) * 3,
        out_specs=(token,) * 2 + (weight,) * 3,
        check_vma=False,
    )
```

```python
import functools

import jax
import jax.numpy as jnp
from jax import lax
from jax.experimental import pallas as pl
from jax.experimental.pallas import tpu as pltpu
from jax.sharding import PartitionSpec as P

BF = jnp.bfloat16
F32 = jnp.float32
T = 128
D = 2048
E = 16
SRC = 32
MAIN = 16
REST = 4
ROWS = SRC * (MAIN + REST)
FULL = SRC * MAIN
CB = 256
MB = 1 << 20


def iota(shape, dim):
    return lax.broadcasted_iota(jnp.int32, shape, dim)


def dot(a, b, ca=1, cb=0):
    return lax.dot_general(a, b, (((ca,), (cb,)), ((), ())), preferred_element_type=F32)


def slots(routes):
    expert = iota((128, T), 0)
    first = routes[0:1, :] == expert
    second = routes[1:2, :] == expert
    member = jnp.logical_or(first, second)
    before = (iota((T, T), 0) < iota((T, T), 1)).astype(F32).astype(BF)
    position = dot(member.astype(F32).astype(BF), before)
    return first, second, jnp.where(member, position, -1.0)


def send_kernel(routes_ref, gates_ref, x_ref, dy_ref, out_ref, made_ref, sem):
    first, second, slot = slots(routes_ref[...])
    gates = gates_ref[...].astype(F32)
    gate = jnp.where(first, gates[0:1, :], 0.0) + jnp.where(second, gates[1:2, :], 0.0)
    count = E * MAIN
    expand = (iota((count, 128), 0) // MAIN == iota((count, 128), 1)).astype(F32).astype(BF)
    slot_row = dot(expand, slot.astype(BF))
    gate_row = dot(expand, gate.astype(BF))
    row = iota((count, T), 0)
    main = slot_row == (row % MAIN).astype(F32)
    rest = slot_row == (row % REST + MAIN).astype(F32)
    block = row // REST % 4

    outs = []
    for which, (values, src_ref) in enumerate(((1.0, x_ref), (gate_row, dy_ref))):
        pick = jnp.where(main, values, 0.0).astype(BF)
        picks = [jnp.where(jnp.logical_and(rest, block == k), values, 0.0).astype(BF) for k in range(4)]
        made = made_ref.at[which]

        def put(at, rows):
            made[:, :, at * MAIN:(at + 1) * MAIN, :] = rows.astype(BF).reshape(E // 2, 2, MAIN, CB)

        for group in range(2):
            left = None
            for k in range(4):
                d = group * 4 + k
                cols = src_ref[:, d * CB:(d + 1) * CB]
                put(d, dot(pick, cols))
                more = dot(picks[k], cols)
                left = more if left is None else left + more
            put(8 + group, left)
        for side in range(2):
            place = out_ref.at[:, side, :, pl.ds(which * 10 * MAIN, 10 * MAIN), :]
            outs.append(pltpu.make_async_copy(made, place, sem.at[which, side]))
            outs[-1].start()
    for copy in outs:
        copy.wait()


def rest_pick(k):
    shape = (SRC * REST, FULL)
    r, c = iota(shape, 0), iota(shape, 1)
    hit = jnp.logical_and(r // REST == c // MAIN, r % REST == c % REST)
    return jnp.logical_and(hit, c // REST % 4 == k).astype(F32).astype(BF)


def unpack(rows_in, base, into, left_ref, sem):
    copies = []
    for d in range(8):
        copies.append(pltpu.make_async_copy(
            rows_in.at[:, pl.ds((base + d) * MAIN, MAIN)],
            into.at[pl.ds(0, SRC), :, pl.ds(d * CB, CB)], sem.at[d]))
    for group in range(2):
        copies.append(pltpu.make_async_copy(
            rows_in.at[:, pl.ds((base + 8 + group) * MAIN, MAIN)], left_ref.at[group], sem.at[8 + group]))
    return copies


def spread_rest(into, left_ref, picks):
    for d in range(8):
        left = left_ref[d // 4].reshape(FULL, CB)
        got = dot(picks[d % 4], left).astype(BF)
        into[SRC:ROWS // MAIN, :, d * CB:(d + 1) * CB] = got.reshape(ROWS // MAIN - SRC, MAIN, CB)


def grad_block(rows_ref, side_ref, cols):
    return dot(rows_ref[:, :, cols].reshape(ROWS, CB), side_ref[...], 0, 0).astype(BF)


def main_kernel(rows_in, w_in, side_out, gate_out, grad_out,
                x_ref, dy_ref, left_ref, w_ref, grad_ref, side_ref, pre_ref, gate_ref,
                x_sem, dy_sem, w_sem, out_sem, end_sem):
    x_copies = unpack(rows_in, 0, x_ref, left_ref.at[0], x_sem)
    dy_copies = unpack(rows_in, 10, dy_ref, left_ref.at[1], dy_sem)
    w_copies = [[[pltpu.make_async_copy(w_in.at[d, q, m], w_ref.at[q, m, d], w_sem.at[q, m, d])
                  for d in range(8)] for m in range(3)] for q in range(2)]
    batches = (
        x_copies + w_copies[0][0],
        w_copies[0][1] + w_copies[1][0] + w_copies[1][1],
        dy_copies + w_copies[0][2] + w_copies[1][2],
    )
    for batch in batches:
        for copy in batch:
            copy.start()
    picks = [rest_pick(k) for k in range(4)]
    for copy in batches[0]:
        copy.wait()
    spread_rest(x_ref, left_ref.at[0], picks)
    pre_ref[0, 0] = dot(x_ref[...].reshape(ROWS, D), w_ref[0, 0].reshape(D, CB))
    for copy in batches[1]:
        copy.wait()
    for q, m in ((0, 1), (1, 0), (1, 1)):
        pre_ref[q, m] = dot(x_ref[...].reshape(ROWS, D), w_ref[q, m].reshape(D, CB))
    for copy in batches[2]:
        copy.wait()
    spread_rest(dy_ref, left_ref.at[1], picks)
    for q in range(2):
        zeta = dot(dy_ref[...].reshape(ROWS, D), w_ref[q, 2].reshape(D, CB))
        gpre, upre = pre_ref[q, 0], pre_ref[q, 1]
        sig = jax.nn.sigmoid(gpre)
        act = gpre * sig
        hidden = (act * upre).astype(BF)
        part = jnp.sum(hidden.astype(F32) * zeta, axis=1, keepdims=True)
        part = jnp.broadcast_to(part, (ROWS, 128))
        gate_ref[...] = part if q == 0 else gate_ref[...] + part
        side_ref[q, 0] = (zeta * upre * sig * (1.0 + gpre * (1.0 - sig))).astype(BF)
        side_ref[q, 1] = (zeta * act).astype(BF)
        side_ref[q, 2] = hidden
    rows_refs = (x_ref, x_ref, dy_ref)
    outs = [pltpu.make_async_copy(gate_ref, gate_out, end_sem.at[0]),
            pltpu.make_async_copy(side_ref.at[:, pl.ds(0, 2)], side_out, end_sem.at[1])]
    for d in range(8):
        cols = slice(d * CB, (d + 1) * CB)
        for q in range(2):
            for m in range(3):
                grad_ref[d, q, m] = grad_block(rows_refs[m], side_ref.at[q, m], cols)
        outs.append(pltpu.make_async_copy(grad_ref.at[d], grad_out.at[d], out_sem.at[d]))
        if d == 1 or d == 3 or d >= 5:
            for copy in outs if d == 1 else outs[-2:] if d < 6 else outs[-1:]:
                copy.start()
    for copy in outs:
        copy.wait()


def back_kernel(w_in, side_in, gate_in, back_out, w_ref, side_ref, gate_ref, back_ref, w_sem, end_sem):
    first = [pltpu.make_async_copy(side_in, side_ref, end_sem.at[0]),
             pltpu.make_async_copy(gate_in, gate_ref, end_sem.at[1])]
    w_copies = [[pltpu.make_async_copy(w_in.at[d, q, m], w_ref.at[q, m, d], w_sem.at[q, m, d])
                 for q in range(2) for m in range(2)] for d in range(8)]
    for copy in first + [copy for copies in w_copies for copy in copies]:
        copy.start()
    picks = [rest_pick(k) for k in range(4)]
    for copy in first:
        copy.wait()
    outs = []

    def put(at):
        rows = (slice(None), pl.ds(at * MAIN, MAIN))
        outs.append(pltpu.make_async_copy(back_ref.at[rows], back_out.at[rows], end_sem.at[2 + at]))
        outs[-1].start()

    gates = gate_ref[...].astype(BF)
    back_ref[:, 10 * MAIN:11 * MAIN, 0:128] = gates[0:FULL].reshape(SRC, MAIN, 128)
    spread = dot(picks[0], gates[FULL:ROWS], 0, 0).astype(BF)
    back_ref[:, 10 * MAIN:11 * MAIN, 128:256] = spread.reshape(SRC, MAIN, 128)
    put(10)
    for group in range(2):
        left = None
        for copies in w_copies[group * 4:group * 4 + 4]:
            for copy in copies:
                copy.wait()
        for k in range(4):
            d = group * 4 + k
            total = dot(side_ref[0, 0], w_ref[0, 0, d], 1, 1) + dot(side_ref[0, 1], w_ref[0, 1, d], 1, 1)
            total += dot(side_ref[1, 0], w_ref[1, 0, d], 1, 1) + dot(side_ref[1, 1], w_ref[1, 1, d], 1, 1)
            rows = total.astype(BF)
            back_ref[:, d * MAIN:(d + 1) * MAIN, :] = rows[0:FULL].reshape(SRC, MAIN, CB)
            more = dot(picks[k], rows[FULL:ROWS], 0, 0)
            left = more if left is None else left + more
        back_ref[:, (8 + group) * MAIN:(9 + group) * MAIN, :] = left.astype(BF).reshape(SRC, MAIN, CB)
        for at in (*range(group * 4, group * 4 + 4), 8 + group):
            put(at)
    for copy in outs:
        copy.wait()


def combine_kernel(routes_ref, gates_ref, back_ref, grad_ref, gate_ref):
    first, second, slot = slots(routes_ref[...])
    gates = gates_ref[...].astype(F32)
    count = 2 * E * MAIN
    place = iota((128, count), 1)
    expand = (place // (4 * MAIN) * 2 + place // MAIN % 2 == iota((128, count), 0)).astype(F32).astype(BF)
    col = iota((T, count), 1)
    main_at = (col % MAIN).astype(F32)
    rest_at = (col % REST + MAIN).astype(F32)
    block = col // REST % 4
    slot_col = dot(slot.astype(BF), expand, 0, 0)
    main = (slot_col == main_at).astype(F32).astype(BF)
    rest = slot_col == rest_at
    rests = [jnp.logical_and(rest, block == k).astype(F32).astype(BF) for k in range(4)]
    for d in range(8):
        got = back_ref[:, d * MAIN:(d + 1) * MAIN, :].reshape(count, CB)
        at = (8 + d // 4) * MAIN
        more = back_ref[:, at:at + MAIN, :].reshape(count, CB)
        grad_ref[:, d * CB:(d + 1) * CB] = (dot(main, got) + dot(rests[d % 4], more)).astype(BF)
    parts = back_ref[:, 10 * MAIN:11 * MAIN, :].reshape(count, CB)
    for k, chosen in enumerate((first, second)):
        own = dot(jnp.where(chosen, slot, -1.0).astype(BF), expand, 0, 0)
        own = jnp.where(dot(chosen.astype(F32).astype(BF), expand, 0, 0) > 0.5, own, -1.0)
        a = (own == main_at).astype(F32).astype(BF)
        b = jnp.logical_and(own == rest_at, block == 0).astype(F32).astype(BF)
        value = dot(parts[:, 0:128], a, 0, 1) + dot(parts[:, 128:256], b, 0, 1)
        gate_ref[k:k + 1, :] = value[0:1, :] / gates[k:k + 1, :]


def vmem(count):
    return [pl.BlockSpec(memory_space=pltpu.VMEM)] * count


def cost(flops, moved):
    return pl.CostEstimate(flops=flops, bytes_accessed=moved, transcendentals=0)


def shape(*sizes, dtype=BF):
    return jax.ShapeDtypeStruct(sizes, dtype)


def call(kernel, name, outs, args, flops, moved, kinds=None, out_kinds=None, scratch=(), limit=63400000):
    spaces = {"s": pltpu.SMEM, "v": pltpu.VMEM, "a": pl.ANY}
    kinds = kinds or "v" * len(args)
    out_kinds = out_kinds or "v" * len(outs)
    return pl.pallas_call(
        kernel,
        out_shape=tuple(outs),
        in_specs=[pl.BlockSpec(memory_space=spaces[k]) for k in kinds],
        out_specs=tuple(pl.BlockSpec(memory_space=spaces[k]) for k in out_kinds),
        scratch_shapes=list(scratch),
        compiler_params=pltpu.CompilerParams(vmem_limit_bytes=limit),
        cost_estimate=cost(flops, moved),
        name=name,
    )(*args)


PARTNER = [(i, i ^ 1) for i in range(SRC)]


def per_device(inputs, cotangent, routes, gate_weights, gate_weight, up_weight, down_weight):
    core = lax.axis_index("eslice") % 2
    dma = pltpu.SemaphoreType.DMA
    mats = (gate_weight, up_weight, down_weight)

    theirs = [lax.ppermute(w, "eslice", PARTNER) for w in mats]
    second = core == 1
    packed = jnp.stack([jnp.where(second, w[1], w[0]) for w in (*mats, *theirs)]).reshape(2, 3, CB, CB)
    weights = lax.all_gather(packed, "dp", axis=0, tiled=False)

    (sent,) = call(send_kernel, "send", [shape(E // 2, 2, 2, 20 * MAIN, CB)],
                   (routes.T, gate_weights.T, inputs, cotangent), 10**9, 6 * MB, kinds="vvvv", out_kinds="a",
                   scratch=(pltpu.VMEM((2, E // 2, 2, 10 * MAIN, CB), BF), dma((2, 2))))
    rows = lax.all_to_all(sent.reshape(SRC, 20 * MAIN, CB), "eslice", 0, 0, tiled=True)

    tiles = pltpu.VMEM((ROWS // MAIN, MAIN, D), BF)
    rests = pltpu.VMEM((2, 2, SRC, MAIN, CB), BF)
    gate_vmem = pltpu.VMEM((ROWS, 128), F32)
    side, gate_part, grads = call(
        main_kernel, "main",
        [shape(2, 2, ROWS, CB), shape(ROWS, 128, dtype=F32), shape(8, 2, 3, CB, CB)],
        (rows, weights), 8 * 10**9, 24 * MB, kinds="aa", out_kinds="aaa",
        scratch=(tiles, tiles, rests, pltpu.VMEM((2, 3, 8, CB, CB), BF),
                 pltpu.VMEM((8, 2, 3, CB, CB), BF), pltpu.VMEM((2, 3, ROWS, CB), BF),
                 pltpu.VMEM((2, 2, ROWS, CB), F32), gate_vmem,
                 dma((10,)), dma((10,)), dma((2, 3, 8)), dma((8,)), dma((2,))))
    reduced = lax.psum_scatter(grads, "dp", scatter_dimension=0, tiled=False)

    (back,) = call(
        back_kernel, "back", [shape(SRC, 11 * MAIN, CB)], (weights, side, gate_part), 3 * 10**9, 10 * MB,
        kinds="aaa", out_kinds="a",
        scratch=(pltpu.VMEM((2, 2, 8, CB, CB), BF), pltpu.VMEM((2, 2, ROWS, CB), BF), gate_vmem,
                 pltpu.VMEM((SRC, 11 * MAIN, CB), BF), dma((2, 2, 8)), dma((13,))))
    returned = lax.all_to_all(back, "eslice", 0, 0, tiled=True)
    input_grad, gate_grad = call(combine_kernel, "combine", [shape(T, D), shape(2, T, dtype=F32)],
                                 (routes.T, gate_weights.T, returned), 10**9, 4 * MB)
    reduced, input_grad = lax.optimization_barrier((reduced, input_grad))
    came = lax.ppermute(reduced, "eslice", PARTNER)
    grads = []
    for m in range(3):
        low, high = (jnp.where(first, reduced[0, m], came[1, m]) for first in (core == 0, second))
        grads.append(jnp.stack((low, high)))
    return (input_grad, gate_grad.T, *grads)


def solution(mesh):
    token = P(("dp", "eslice"), None)
    weight = P("eslice", "dp", None)
    return jax.shard_map(
        per_device,
        mesh=mesh,
        in_specs=(token,) * 4 + (weight,) * 3,
        out_specs=(token,) * 2 + (weight,) * 3,
        check_vma=False,
    )
```
